32 devices in a mesh: aux: 4 (over x, core), orb: 8 (over z, y).
Axes of the slice: x: 2, y: 2, z: 4, core: 2. Of those that a mesh axis runs over, the one named last changes fastest.
Arguments:
- three_center: float32 [16, 8, 128, 1024], P('aux', 'orb'), may hold values from -6 to 6
- tile_lists: int32 [2, 4, 8, 8], P(None, 'aux'), may hold values from -1 to 7, as said below
- occ_density: float32 [2, 1024, 1024], P(None, 'orb', 'aux'), may hold values from -0.1875 to 0.1875
- vir_density: float32 [2, 1024, 1024], P(None, 'orb', 'aux'), may hold values from -0.1875 to 0.1875
Outputs:
- coupled: float32 [2, 16, 8, 1024, 128], P(None, 'aux', 'orb')
The draws below stay inside these ranges and needn't reach their ends.
Inputs may be any that keep to these rules, and one draw needn't show every extreme that they name: Row m of tile_lists[t, j] names distinct orbital blocks in rising order, block m always among them, and -1 in the remaining places; it names between 2 and 8 blocks, and for every t and j one row names all 8 and another exactly 2.
All inputs are finite; a program needn't handle non-finite values.
Results may differ from the reference program's by a relative error of at most 0.0003.
Values sent between devices are 32-bit elements; how exact they have to be, the bound alone decides.
No kernel may reach another device: no remote copies, remote signals or barrier semaphores. Data moves between devices by JAX's collectives and lax.ppermute only.
A program may use at most 64 MiB of HBM per device.

```python
import jax
import jax.numpy as jnp
from jax import lax

ORB = 1024
BLK = 128
AUX_Q = 4
TIMES = 2
NB = 8
ABLOCKS = 4
AUX_ROWS = 16
N_AUX = 4
N_ORB = 8


def draw_tile_lists(key, part):
    group_total = TIMES * ABLOCKS
    row_total = group_total * NB
    base = jax.random.fold_in(key, 7)
    key_count, key_full, key_low, key_score = jax.random.split(base, 4)
    counts = jax.random.randint(key_count, (row_total,), 2, NB + 1)
    full_pick = jax.random.randint(key_full, (group_total,), 0, NB)
    low_pick = (full_pick + 1 + jax.random.randint(key_low, (group_total,), 0, NB - 1)) % NB
    positions = jnp.arange(row_total, dtype=jnp.int32)
    within = positions % NB
    group_ids = positions // NB
    counts = jnp.where(within == full_pick[group_ids], NB, counts)
    counts = jnp.where(within == low_pick[group_ids], 2, counts)
    block_ids = jnp.arange(NB, dtype=jnp.int32)
    scores = jax.random.randint(key_score, (row_total, NB), 0, 1048576) * NB + block_ids[None, :]
    scores = jnp.where(block_ids[None, :] == within[:, None], -1, scores)
    ordering = jnp.argsort(scores, axis=1, stable=True)
    ranking = jnp.argsort(ordering, axis=1, stable=True)
    chosen = ranking < counts[:, None]
    sort_key = jnp.where(chosen, block_ids[None, :], NB + block_ids[None, :])
    listed = jnp.sort(sort_key, axis=1)
    listed = jnp.where(listed < NB, listed, -1)
    return listed.reshape(TIMES, ABLOCKS, NB, NB).astype(jnp.int32)


def steps_of(rng, dims, shards, smallest, top_value):
    factor_of = 1.0
    for axis_at, parts in shards:
        draws = jax.random.uniform(jax.random.fold_in(jax.random.fold_in(rng, 6), axis_at), (parts,), jnp.float32, smallest / len(shards), top_value / len(shards))
        factor_of = factor_of * jnp.repeat(jnp.exp(draws), dims[axis_at] // parts).reshape((-1,) + (1,) * (len(dims) - 1 - axis_at))
    return factor_of


def gaussian(rng, dims, spread, limit, cuts=(), kind=jnp.bfloat16):
    array = spread * jax.random.normal(rng, dims, jnp.float32)
    if cuts:
        array = array * steps_of(rng, dims, cuts, -0.22, 0.18)
    return jnp.clip(array, -limit, limit).astype(kind)


def setup_inputs(seed: int = 0) -> dict:
    splits = jax.random.split(jax.random.key(seed), 5)
    return {
        "three_center": gaussian(splits[0], (AUX_ROWS, N_ORB, BLK, ORB), 1.0, 6.0, ((0, 4), (1, 8)), jnp.float32),
        "tile_lists": draw_tile_lists(jax.random.fold_in(splits[4], 71), 0),
        "occ_density": gaussian(splits[2], (TIMES, ORB, ORB), ORB ** -0.5, 0.1875, ((1, 8), (2, 4)), jnp.float32),
        "vir_density": gaussian(splits[3], (TIMES, ORB, ORB), ORB ** -0.5, 0.1875, ((1, 8), (2, 4)), jnp.float32),
    }


def reference(three_center, tile_lists, occ_density, vir_density):
    block_count = ORB // BLK
    split_count = N_ORB // block_count
    aux_share = AUX_Q // split_count
    grouped = three_center.reshape(N_AUX, AUX_Q, block_count, split_count, BLK, ORB)
    block_ids = jnp.arange(block_count, dtype=jnp.int32)
    outputs = []
    for moment in range(TIMES):
        occ_now = occ_density[moment]
        vir_now = vir_density[moment]

        def per_block(inputs):
            block_number, listed_rows = inputs
            column = block_number // split_count
            part_number = block_number % split_count
            chosen = lax.dynamic_index_in_dim(grouped, column, 0, keepdims=False)
            chosen = lax.dynamic_index_in_dim(chosen, part_number, 2, keepdims=False)
            integrals = chosen.reshape(AUX_Q, ORB, ORB)
            matches = listed_rows[:, :, None] == block_ids[None, None, :]
            listed = jnp.sum(matches.astype(jnp.float32), axis=1)
            tile_keep = jnp.repeat(jnp.repeat(listed, BLK, axis=0), BLK, axis=1)
            masked = integrals * tile_keep[None]
            half = jnp.dot(masked.reshape(AUX_Q * ORB, ORB), occ_now,
                           precision=lax.Precision.HIGHEST,
                           preferred_element_type=jnp.float32).reshape(AUX_Q, ORB, ORB)
            half = half * tile_keep[None]
            full = jnp.einsum("sk,akl->asl", vir_now, half, precision=lax.Precision.HIGHEST)
            arranged = full.reshape(split_count, aux_share, ORB, block_count, BLK)
            arranged = arranged.transpose(1, 3, 0, 2, 4)
            return arranged.reshape(aux_share, N_ORB, ORB, BLK)

        block_numbers = jnp.arange(N_AUX * split_count, dtype=jnp.int32)
        blocks = lax.map(per_block, (block_numbers, tile_lists[moment]))
        outputs.append(blocks.reshape(N_AUX * AUX_Q, N_ORB, ORB, BLK))
    return jnp.stack(outputs, axis=0)
```

```python
import functools

import jax
import jax.numpy as jnp
from jax import lax
from jax.experimental import pallas as pl
from jax.experimental.pallas import tpu as pltpu
from jax.sharding import PartitionSpec as P

VMEM_BYTES = 56 * 1024 * 1024


def listed_mask(tile_lists, part_index, block_index):
    block_table = lax.dynamic_index_in_dim(tile_lists, part_index, 1, keepdims=False)
    listed_row = lax.dynamic_index_in_dim(block_table, block_index, 1, keepdims=False)
    block_ids = jnp.arange(tile_lists.shape[3], dtype=jnp.int32)
    matches = listed_row[:, :, None] == block_ids[None, None, :]
    return jnp.sum(matches.astype(jnp.float32), axis=1)


def halves(value):
    high = value.astype(jnp.bfloat16)
    return high, (value - high.astype(jnp.float32)).astype(jnp.bfloat16)


def three_products(left_high, left_low, right_high, right_low):
    dot = functools.partial(jnp.dot, preferred_element_type=jnp.float32)
    small = dot(left_low, right_high) + dot(left_high, right_low)
    return dot(left_high, right_high) + small


def exchange(value, aux_bits, orb_bits):
    n_aux, n_orb = lax.axis_size("aux"), lax.axis_size("orb")
    pairs = [
        (a * n_orb + o, (a ^ aux_bits) * n_orb + (o ^ orb_bits))
        for a in range(n_aux)
        for o in range(n_orb)
    ]
    return lax.ppermute(value, ("aux", "orb"), pairs)


def bits_of(size):
    return [1 << at for at in reversed(range(size.bit_length() - 1))]


def gather(value):
    stacked, keys = value[None], [(0, 0)]
    for bit in bits_of(lax.axis_size("orb")):
        stacked = jnp.concatenate([stacked, exchange(stacked, 0, bit)], axis=0)
        keys = keys + [(a, o ^ bit) for a, o in keys]
    gathered = [(stacked, keys)]
    for bit in bits_of(lax.axis_size("aux")):
        gathered = gathered + [
            (exchange(array, bit, 0), [(a ^ bit, o) for a, o in names]) for array, names in gathered
        ]
    return gathered


def place_blocks(position, refs, keys, high_ref, low_ref):
    my_aux, my_orb = position[0], position[1]
    for ref, names in zip(refs, keys):
        rows, cols = ref.shape[1:]
        for at, (aux_bits, orb_bits) in enumerate(names):
            row = pl.multiple_of((my_orb ^ orb_bits) * rows, rows)
            col = pl.multiple_of((my_aux ^ aux_bits) * cols, cols)
            high, low = halves(ref[at])
            high_ref[pl.ds(row, rows), pl.ds(col, cols)] = high
            low_ref[pl.ds(row, rows), pl.ds(col, cols)] = low


def half_kernel(keys, time, split, position, listed, integrals, *rest):
    refs, (out, b_high, b_low, a_high, a_low) = rest[: len(keys)], rest[len(keys) :]
    aux_count, block, orbitals = integrals.shape
    blocks = orbitals // block
    share = aux_count // split
    place_blocks(position, refs, keys, b_high, b_low)
    for n in range(blocks):
        cols = slice(n * block, (n + 1) * block)
        part = integrals[:, :, cols].reshape(aux_count * block, block) * listed[time, n]
        a_high[:, cols], a_low[:, cols] = halves(part)
    width = 2 * block
    for pair in range(blocks // 2):
        cols = slice(pair * width, (pair + 1) * width)
        product = three_products(a_high[...], a_low[...], b_high[:, cols], b_low[:, cols])
        for side in range(2):
            column = pair * 2 + side
            part = product[:, side * block : (side + 1) * block] * listed[time, column]
            part = part.reshape(split, share, block, block)
            for h in range(split):
                out[(column * split + h) ^ position[1]] = part[h]


def half_products(position, listed, integrals, gathered, time, split):
    arrays, keys = [g[0] for g in gathered], [g[1] for g in gathered]
    aux_count, block, orbitals = integrals.shape
    units = orbitals // block * split
    smem = pl.BlockSpec(memory_space=pltpu.SMEM)
    vmem = pl.BlockSpec(memory_space=pltpu.VMEM)
    return pl.pallas_call(
        functools.partial(half_kernel, keys, time, split),
        out_shape=jax.ShapeDtypeStruct((units, aux_count // split, block, block), jnp.float32),
        in_specs=[smem, smem, vmem] + [vmem] * len(arrays),
        out_specs=vmem,
        scratch_shapes=[pltpu.VMEM((orbitals, orbitals), jnp.bfloat16)] * 2
        + [pltpu.VMEM((aux_count * block, orbitals), jnp.bfloat16)] * 2,
        compiler_params=pltpu.CompilerParams(vmem_limit_bytes=VMEM_BYTES),
        cost_estimate=pl.CostEstimate(
            flops=6 * aux_count * block * orbitals * orbitals,
            bytes_accessed=4 * (orbitals * orbitals + 2 * aux_count * block * orbitals),
            transcendentals=0,
        ),
        name="half_products",
    )(position, listed, integrals, *arrays)


def split_kernel(keys, position, *rest):
    refs, (high, low) = rest[: len(keys)], rest[len(keys) :]
    place_blocks(position, refs, keys, high, low)


def split_whole(position, gathered, orbitals):
    arrays, keys = [g[0] for g in gathered], [g[1] for g in gathered]
    smem = pl.BlockSpec(memory_space=pltpu.SMEM)
    vmem = pl.BlockSpec(memory_space=pltpu.VMEM)
    return pl.pallas_call(
        functools.partial(split_kernel, keys),
        out_shape=[jax.ShapeDtypeStruct((orbitals, orbitals), jnp.bfloat16)] * 2,
        in_specs=[smem] + [vmem] * len(arrays),
        out_specs=[vmem] * 2,
        compiler_params=pltpu.CompilerParams(vmem_limit_bytes=VMEM_BYTES),
        cost_estimate=pl.CostEstimate(
            flops=4 * orbitals * orbitals, bytes_accessed=8 * orbitals * orbitals, transcendentals=0
        ),
        name="split_whole",
    )(position, *arrays)


def full_kernel(split, count, position, a_high, a_low, own, *rest):
    received, (out, b_high, b_low) = rest[: count - 1], rest[-3:]
    share, block, _ = own.shape[1:]
    for bits in range(count):
        source = position[1] ^ bits
        row = pl.multiple_of(source // split * block, block)
        for at in range(share):
            value = own[0, at] if bits == 0 else received[bits - 1][at]
            col = pl.multiple_of((source % split * share + at) * block, block)
            high, low = halves(value)
            b_high[pl.ds(row, block), pl.ds(col, block)] = high
            b_low[pl.ds(row, block), pl.ds(col, block)] = low
    orbitals = a_high.shape[0]
    tile = 2 * block
    for start in range(0, orbitals, tile):
        rows = slice(start, start + tile)
        product = three_products(a_high[rows], a_low[rows], b_high[...], b_low[...])
        for at in range(share * split):
            out[0, at, 0, rows] = product[:, at * block : (at + 1) * block]


def full_products(position, vir, own, received, time, times, split, earlier):
    high, low = vir
    orbitals = high.shape[0]
    units, share, block, _ = own.shape
    aux_count = share * split
    smem = pl.BlockSpec(memory_space=pltpu.SMEM)
    vmem = pl.BlockSpec(memory_space=pltpu.VMEM)
    first = pl.BlockSpec((1, share, block, block), lambda i: (0, 0, 0, 0))
    operands = [position, high, low, own, *received]
    in_specs = [smem, vmem, vmem, first] + [vmem] * len(received)
    aliases = {}
    if earlier is not None:
        aliases = {len(operands): 0}
        operands.append(earlier)
        in_specs.append(pl.BlockSpec(memory_space=pl.ANY))
    return pl.pallas_call(
        functools.partial(full_kernel, split, units),
        grid=(1,),
        out_shape=jax.ShapeDtypeStruct((times, aux_count, 1, orbitals, block), jnp.float32),
        in_specs=in_specs,
        out_specs=pl.BlockSpec((1, aux_count, 1, orbitals, block), lambda i: (time, 0, 0, 0, 0)),
        scratch_shapes=[pltpu.VMEM((orbitals, aux_count * block), jnp.bfloat16)] * 2,
        input_output_aliases=aliases,
        compiler_params=pltpu.CompilerParams(vmem_limit_bytes=VMEM_BYTES),
        cost_estimate=pl.CostEstimate(
            flops=6 * aux_count * block * orbitals * orbitals,
            bytes_accessed=4 * (orbitals * orbitals + 2 * aux_count * block * orbitals),
            transcendentals=0,
        ),
        name="full_products",
    )(*operands)


def local(three_center, tile_lists, occ_density, vir_density):
    integrals = three_center[:, 0]
    block, orbitals = three_center.shape[2:]
    owners = lax.axis_size("orb")
    split = owners // (orbitals // block)
    unit = lax.axis_index("orb")
    listed = listed_mask(tile_lists, unit % split, unit // split)
    position = jnp.stack([lax.axis_index("aux"), unit]).astype(jnp.int32)
    times = occ_density.shape[0]
    sent, received = [], []
    for time in range(times):
        gathered = gather(occ_density[time])
        products = half_products(position, listed, integrals, gathered, time, split)
        sent.append(products)
        received.append([exchange(products[bits], 0, bits) for bits in range(1, owners)])
    coupled = None
    for time in range(times):
        vir = split_whole(position, gather(vir_density[time]), orbitals)
        coupled = full_products(
            position, vir, sent[time], received[time], time, times, split, coupled
        )
    return coupled


def solution(mesh):
    in_specs = (
        P("aux", "orb", None, None),
        P(None, "aux", None, None),
        P(None, "orb", "aux"),
        P(None, "orb", "aux"),
    )
    out_specs = P(None, "aux", "orb", None, None)
    return jax.shard_map(local, mesh=mesh, in_specs=in_specs, out_specs=out_specs, check_vma=False)
```

```python
import functools

import jax
import jax.numpy as jnp
from jax import lax
from jax.experimental import pallas as pl
from jax.experimental.pallas import tpu as pltpu
from jax.sharding import PartitionSpec as P

VMEM_BYTES = 56 * 1024 * 1024
SMEM = pl.BlockSpec(memory_space=pltpu.SMEM)
VMEM = pl.BlockSpec(memory_space=pltpu.VMEM)
PARAMS = pltpu.CompilerParams(vmem_limit_bytes=VMEM_BYTES)


def cost(flops, moved):
    return pl.CostEstimate(flops=flops, bytes_accessed=moved, transcendentals=0)


def listed_mask(tile_lists, part_index, block_index):
    block_table = lax.dynamic_index_in_dim(tile_lists, part_index, 1, keepdims=False)
    listed_row = lax.dynamic_index_in_dim(block_table, block_index, 1, keepdims=False)
    block_ids = jnp.arange(tile_lists.shape[3], dtype=jnp.int32)
    matches = listed_row[:, :, None] == block_ids[None, None, :]
    return jnp.sum(matches.astype(jnp.float32), axis=1)


def halves(value):
    high = value.astype(jnp.bfloat16)
    return high, (value - high.astype(jnp.float32)).astype(jnp.bfloat16)


def three_products(left_high, left_low, right_high, right_low):
    dot = functools.partial(jnp.dot, preferred_element_type=jnp.float32)
    small = dot(left_low, right_high) + dot(left_high, right_low)
    return dot(left_high, right_high) + small


def after(value, *others):
    return lax.optimization_barrier((value, *others))[0]


def permute(value, target):
    n_aux, n_orb = lax.axis_size("aux"), lax.axis_size("orb")
    pairs = []
    for a in range(n_aux):
        for o in range(n_orb):
            to_aux, to_orb = target(a, o)
            pairs.append((a * n_orb + o, to_aux * n_orb + to_orb))
    return lax.ppermute(value, ("aux", "orb"), pairs)


def swap(value, aux_bits=0, orb_bits=0):
    return permute(value, lambda a, o: (a ^ aux_bits, o ^ orb_bits))


def together(*gathers):
    arrays = [array for g in gathers for array in (g.arrays() if isinstance(g, Gather) else g)]
    arrays = list(lax.optimization_barrier(tuple(arrays)))
    found = [g for g in gathers if isinstance(g, Gather)]
    return [Gather([(arrays.pop(0), keys) for keys in g.keys()]) for g in found]


def bits_of(size):
    return [1 << at for at in reversed(range(size.bit_length() - 1))]


class Gather:
    def __init__(self, parts):
        self.parts = parts

    def step(self, aux_bits=0, orb_bits=0, stack=True):
        parts = list(self.parts)
        for array, keys in self.parts:
            got = swap(array, aux_bits, orb_bits)
            names = [(a ^ aux_bits, o ^ orb_bits if orb_bits else o) for a, o in keys]
            if stack:
                parts = [(jnp.concatenate([array, got], axis=0), keys + names)]
            else:
                parts.append((got, names))
        return Gather(parts)

    def rows(self, start, stop):
        return Gather([(array[:, start:stop], keys) for array, keys in self.parts])

    def at(self, time):
        return Gather([(array[:, time], keys) for array, keys in self.parts])

    def after(self, *others):
        return Gather([(after(array, *others), keys) for array, keys in self.parts])

    def arrays(self):
        return [array for array, _ in self.parts]

    def keys(self):
        return [keys for _, keys in self.parts]


def owner_of(my_orb, key):
    return key[0] if isinstance(key, tuple) else my_orb ^ key


def split_integrals_kernel(listed, integrals, *outs):
    aux_count, block, orbitals = integrals.shape
    for n in range(orbitals // block):
        cols = slice(n * block, (n + 1) * block)
        part = integrals[:, :, cols].reshape(aux_count * block, block)
        for time in range(listed.shape[0]):
            outs[2 * time][:, cols], outs[2 * time + 1][:, cols] = halves(part * listed[time, n])


def split_integrals(listed, integrals):
    aux_count, block, orbitals = integrals.shape
    times = listed.shape[0]
    shape = jax.ShapeDtypeStruct((aux_count * block, orbitals), jnp.bfloat16)
    return pl.pallas_call(
        split_integrals_kernel,
        out_shape=[shape] * (2 * times),
        in_specs=[SMEM, VMEM],
        out_specs=[VMEM] * (2 * times),
        compiler_params=PARAMS,
        cost_estimate=cost(8 * aux_count * block * orbitals, 12 * aux_count * block * orbitals),
        name="split_integrals",
    )(listed, integrals)


def half_kernel(keys, time, split, position, listed, a_high, a_low, *rest):
    refs, (out, b_high, b_low) = rest[: len(keys)], rest[len(keys) :]
    my_aux, my_orb = position[0], position[1]
    _, share, block, _ = out.shape
    for ref, (names, offset, stride) in zip(refs, keys):
        rows, cols = ref.shape[1:]
        for at, (aux_bits, orb_bits) in enumerate(names):
            row = pl.multiple_of(owner_of(my_orb, orb_bits) * stride + offset, rows)
            col = pl.multiple_of((my_aux ^ aux_bits) * cols, cols)
            high, low = halves(ref[at])
            b_high[pl.ds(row, rows), pl.ds(col, cols)] = high
            b_low[pl.ds(row, rows), pl.ds(col, cols)] = low
    width = 2 * block
    for pair in range(b_high.shape[1] // width):
        cols = slice(pair * width, (pair + 1) * width)
        product = three_products(a_high[...], a_low[...], b_high[:, cols], b_low[:, cols])
        for side in range(2):
            column = pair * 2 + side
            part = product[:, side * block : (side + 1) * block] * listed[time, column]
            part = part.reshape(split, share, block, block)
            for h in range(split):
                out[column * split + h] = part[h]


def half_products(position, listed, a_split, sources, time, split, block):
    a_high, a_low = a_split
    rows, orbitals = a_high.shape
    aux_count = rows // block
    shape = (orbitals // block * split, aux_count // split, block, block)
    arrays, keys = [], []
    for gathered, offset, stride in sources:
        for array, names in gathered.parts:
            arrays.append(array)
            keys.append((names, offset, stride))
    return pl.pallas_call(
        functools.partial(half_kernel, keys, time, split),
        out_shape=jax.ShapeDtypeStruct(shape, jnp.float32),
        in_specs=[SMEM, SMEM, VMEM, VMEM] + [VMEM] * len(arrays),
        out_specs=VMEM,
        scratch_shapes=[pltpu.VMEM((orbitals, orbitals), jnp.bfloat16)] * 2,
        compiler_params=PARAMS,
        cost_estimate=cost(6 * aux_count * block * orbitals * orbitals, 10 * orbitals * orbitals),
        name="half_products",
    )(position, listed, a_high, a_low, *arrays)


def split_kernel(keys, position, *rest):
    refs, (high_ref, low_ref) = rest[: len(keys)], rest[len(keys) :]
    my_aux, my_orb = position[0], position[1]
    for ref, names in zip(refs, keys):
        rows, cols = ref.shape[1:]
        for at, (aux_bits, orb_bits) in enumerate(names):
            row = pl.multiple_of(owner_of(my_orb, orb_bits) * rows, rows)
            col = pl.multiple_of((my_aux ^ aux_bits) * cols, cols)
            high, low = halves(ref[at])
            high_ref[pl.ds(row, rows), pl.ds(col, cols)] = high
            low_ref[pl.ds(row, rows), pl.ds(col, cols)] = low


def split_whole(position, gathered, orbitals):
    return pl.pallas_call(
        functools.partial(split_kernel, gathered.keys()),
        out_shape=[jax.ShapeDtypeStruct((orbitals, orbitals), jnp.bfloat16)] * 2,
        in_specs=[SMEM] + [VMEM] * len(gathered.parts),
        out_specs=[VMEM] * 2,
        compiler_params=PARAMS,
        cost_estimate=cost(4 * orbitals * orbitals, 8 * orbitals * orbitals),
        name="split_whole",
    )(position, *gathered.arrays())


def full_kernel(split, a_high, a_low, received, *rest):
    out, b_high, b_low = rest[-3:]
    units, share, block, _ = received.shape
    for source in range(units):
        rows = slice(source // split * block, (source // split + 1) * block)
        for at in range(share):
            col = (source % split * share + at) * block
            b_high[rows, col : col + block], b_low[rows, col : col + block] = halves(received[source, at])
    orbitals = a_high.shape[0]
    tile = 2 * block
    for start in range(0, orbitals, tile):
        rows = slice(start, start + tile)
        product = three_products(a_high[rows], a_low[rows], b_high[...], b_low[...])
        for at in range(share * split):
            out[0, at, 0, rows] = product[:, at * block : (at + 1) * block]


def full_products(vir, received, time, times, split, earlier):
    high, low = vir
    orbitals = high.shape[0]
    units, share, block, _ = received.shape
    aux_count = share * split
    operands = [high, low, received]
    in_specs = [VMEM] * 3
    aliases = {}
    if earlier is not None:
        aliases = {len(operands): 0}
        operands.append(earlier)
        in_specs.append(pl.BlockSpec(memory_space=pl.ANY))
    return pl.pallas_call(
        functools.partial(full_kernel, split),
        grid=(1,),
        out_shape=jax.ShapeDtypeStruct((times, aux_count, 1, orbitals, block), jnp.float32),
        in_specs=in_specs,
        out_specs=pl.BlockSpec((1, aux_count, 1, orbitals, block), lambda i: (time, 0, 0, 0, 0)),
        scratch_shapes=[pltpu.VMEM((orbitals, aux_count * block), jnp.bfloat16)] * 2,
        input_output_aliases=aliases,
        compiler_params=PARAMS,
        cost_estimate=cost(6 * aux_count * block * orbitals * orbitals, 12 * orbitals * orbitals),
        name="full_products",
    )(*operands)


def local(three_center, tile_lists, occ_density, vir_density):
    integrals = three_center.reshape(three_center.shape[0], *three_center.shape[2:])
    block, orbitals = three_center.shape[2:]
    owners, n_aux = lax.axis_size("orb"), lax.axis_size("aux")
    split = owners // (orbitals // block)
    unit = lax.axis_index("orb")
    position = jnp.stack([lax.axis_index("aux"), unit]).astype(jnp.int32)
    times = occ_density.shape[0]
    orb_bits, aux_bits = bits_of(owners), bits_of(n_aux)
    core_bit, far_bits = aux_bits[-1], aux_bits[:-1]

    listed = listed_mask(tile_lists, unit % split, unit // split)
    a_split = split_integrals(listed, integrals)

    half_rows = occ_density.shape[1] // 2

    def begin(value):
        return Gather([(value[None], [(0, 0)])])

    def products(sources, time):
        pair = a_split[2 * time : 2 * time + 2]
        return half_products(position, listed, pair, sources, time, split, block)

    def deliver(made):
        return lax.all_to_all(made, "orb", split_axis=0, concat_axis=0, tiled=True)

    far_orb, middle_orb, near_orb = orb_bits[0], orb_bits[1:-1], orb_bits[-1]

    def over_orb(value):
        whole = lax.all_gather(value, "orb", axis=0)
        return Gather([(whole, [(0, (owner,)) for owner in range(owners)])])

    begun = begin(occ_density[0]).step(orb_bits=far_orb)
    begun = together(begun, a_split)[0]
    one, two = begun.rows(0, half_rows), begun.rows(half_rows, 2 * half_rows)
    for bit in middle_orb:
        one = one.step(orb_bits=bit)
    for bit in far_bits:
        two = two.step(aux_bits=bit)
    one, two = together(one, two)
    rest = over_orb(jnp.concatenate([occ_density[1:], vir_density], axis=0))
    one = one.step(orb_bits=near_orb)
    for bit in middle_orb:
        two = two.step(orb_bits=bit)
    for bit in far_bits:
        one = one.step(aux_bits=bit, stack=False)
    two = two.step(orb_bits=near_orb, stack=False)
    one = one.step(aux_bits=core_bit, stack=False)
    two = two.step(aux_bits=core_bit, stack=False)
    sources = [(one, 0, 2 * half_rows), (two, half_rows, 2 * half_rows)]
    made = products(sources, 0)
    received = [deliver(made)]
    rest = rest.after(made)

    def cross(gathered):
        for bit in far_bits:
            gathered = gathered.step(aux_bits=bit, stack=False)
        return gathered

    def finish(gathered):
        return gathered.step(aux_bits=core_bit, stack=False)

    for time in range(1, times):
        made = products([(finish(cross(rest.at(time - 1))), 0, 2 * half_rows)], time)
        received.append(deliver(made))
    virs = [cross(rest.at(times - 1 + time)) for time in range(times)]
    coupled = None
    for time in range(times):
        gathered = virs[time] if coupled is None else virs[time].after(coupled)
        whole = split_whole(position, finish(gathered), orbitals)
        coupled = full_products(whole, received[time], time, times, split, coupled)
    return coupled


def solution(mesh):
    in_specs = (
        P("aux", "orb", None, None),
        P(None, "aux", None, None),
        P(None, "orb", "aux"),
        P(None, "orb", "aux"),
    )
    out_specs = P(None, "aux", "orb", None, None)
    return jax.shard_map(local, mesh=mesh, in_specs=in_specs, out_specs=out_specs, check_vma=False)
```

```python
import functools

import jax
import jax.numpy as jnp
from jax import lax
from jax.experimental import pallas as pl
from jax.experimental.pallas import tpu as pltpu
from jax.sharding import PartitionSpec as P

VMEM_BYTES = 56 * 1024 * 1024
SMEM = pl.BlockSpec(memory_space=pltpu.SMEM)
VMEM = pl.BlockSpec(memory_space=pltpu.VMEM)
PARAMS = pltpu.CompilerParams(vmem_limit_bytes=VMEM_BYTES)


def cost(flops, moved):
    return pl.CostEstimate(flops=flops, bytes_accessed=moved, transcendentals=0)


def listed_mask(tile_lists, part_index, block_index):
    block_table = lax.dynamic_index_in_dim(tile_lists, part_index, 1, keepdims=False)
    listed_row = lax.dynamic_index_in_dim(block_table, block_index, 1, keepdims=False)
    block_ids = jnp.arange(tile_lists.shape[3], dtype=jnp.int32)
    matches = listed_row[:, :, None] == block_ids[None, None, :]
    return jnp.sum(matches.astype(jnp.float32), axis=1)


def halves(value):
    high = value.astype(jnp.bfloat16)
    return high, (value - high.astype(jnp.float32)).astype(jnp.bfloat16)


def three_products(left_high, left_low, right_high, right_low):
    dot = functools.partial(jnp.dot, preferred_element_type=jnp.float32)
    small = dot(left_low, right_high) + dot(left_high, right_low)
    return dot(left_high, right_high) + small


def after(value, *others):
    return lax.optimization_barrier((value, *others))[0]


def permute(value, target):
    n_aux, n_orb = lax.axis_size("aux"), lax.axis_size("orb")
    pairs = []
    for a in range(n_aux):
        for o in range(n_orb):
            to_aux, to_orb = target(a, o)
            pairs.append((a * n_orb + o, to_aux * n_orb + to_orb))
    return lax.ppermute(value, ("aux", "orb"), pairs)


def swap(value, aux_bits=0, orb_bits=0):
    return permute(value, lambda a, o: (a ^ aux_bits, o ^ orb_bits))


def together(*values):
    parts = [value.arrays() if isinstance(value, Gather) else [value] for value in values]
    arrays = list(lax.optimization_barrier(tuple(array for part in parts for array in part)))
    found = []
    for value in values:
        if isinstance(value, Gather):
            found.append(Gather([(arrays.pop(0), keys) for keys in value.keys()]))
        else:
            found.append(arrays.pop(0))
    return found


def bits_of(size):
    return [1 << at for at in reversed(range(size.bit_length() - 1))]


class Gather:
    def __init__(self, parts):
        self.parts = parts

    def step(self, aux_bits=0, orb_bits=0, stack=True):
        parts = list(self.parts)
        for array, keys in self.parts:
            got = swap(array, aux_bits, orb_bits)
            names = [(a ^ aux_bits, o ^ orb_bits if orb_bits else o) for a, o in keys]
            if stack:
                parts = [(jnp.concatenate([array, got], axis=0), keys + names)]
            else:
                parts.append((got, names))
        return Gather(parts)

    def rows(self, start, stop):
        return Gather([(array[:, start:stop], keys) for array, keys in self.parts])

    def at(self, time):
        return Gather([(array[:, time], keys) for array, keys in self.parts])

    def after(self, *others):
        return Gather([(after(array, *others), keys) for array, keys in self.parts])

    def arrays(self):
        return [array for array, _ in self.parts]

    def keys(self):
        return [keys for _, keys in self.parts]


def owner_of(my_orb, key):
    return key[0] if isinstance(key, tuple) else my_orb ^ key


def split_integrals_kernel(listed, integrals, *outs):
    aux_count, block, orbitals = integrals.shape
    for n in range(orbitals // block):
        cols = slice(n * block, (n + 1) * block)
        part = integrals[:, :, cols].reshape(aux_count * block, block)
        for time in range(listed.shape[0]):
            outs[2 * time][:, cols], outs[2 * time + 1][:, cols] = halves(part * listed[time, n])


def split_integrals(listed, integrals):
    aux_count, block, orbitals = integrals.shape
    times = listed.shape[0]
    shape = jax.ShapeDtypeStruct((aux_count * block, orbitals), jnp.bfloat16)
    return pl.pallas_call(
        split_integrals_kernel,
        out_shape=[shape] * (2 * times),
        in_specs=[SMEM, VMEM],
        out_specs=[VMEM] * (2 * times),
        compiler_params=PARAMS,
        cost_estimate=cost(8 * aux_count * block * orbitals, 12 * aux_count * block * orbitals),
        name="split_integrals",
    )(listed, integrals)


def half_kernel(keys, time, split, position, listed, a_high, a_low, *rest):
    refs, (out, b_high, b_low) = rest[: len(keys)], rest[len(keys) :]
    my_aux, my_orb = position[0], position[1]
    _, share, block, _ = out.shape
    for ref, (names, offset, stride) in zip(refs, keys):
        rows, cols = ref.shape[1:]
        for at, (aux_bits, orb_bits) in enumerate(names):
            row = pl.multiple_of(owner_of(my_orb, orb_bits) * stride + offset, rows)
            col = pl.multiple_of((my_aux ^ aux_bits) * cols, cols)
            high, low = halves(ref[at])
            b_high[pl.ds(row, rows), pl.ds(col, cols)] = high
            b_low[pl.ds(row, rows), pl.ds(col, cols)] = low
    width = 2 * block
    for pair in range(b_high.shape[1] // width):
        cols = slice(pair * width, (pair + 1) * width)
        product = three_products(a_high[...], a_low[...], b_high[:, cols], b_low[:, cols])
        for side in range(2):
            column = pair * 2 + side
            part = product[:, side * block : (side + 1) * block] * listed[time, column]
            part = part.reshape(split, share, block, block)
            for h in range(split):
                out[column * split + h] = part[h]


def half_products(position, listed, a_split, sources, time, split, block):
    a_high, a_low = a_split
    rows, orbitals = a_high.shape
    aux_count = rows // block
    shape = (orbitals // block * split, aux_count // split, block, block)
    arrays, keys = [], []
    for gathered, offset, stride in sources:
        for array, names in gathered.parts:
            arrays.append(array)
            keys.append((names, offset, stride))
    return pl.pallas_call(
        functools.partial(half_kernel, keys, time, split),
        out_shape=jax.ShapeDtypeStruct(shape, jnp.float32),
        in_specs=[SMEM, SMEM, VMEM, VMEM] + [VMEM] * len(arrays),
        out_specs=VMEM,
        scratch_shapes=[pltpu.VMEM((orbitals, orbitals), jnp.bfloat16)] * 2,
        compiler_params=PARAMS,
        cost_estimate=cost(6 * aux_count * block * orbitals * orbitals, 10 * orbitals * orbitals),
        name="half_products",
    )(position, listed, a_high, a_low, *arrays)


def place_kernel(keys, span, position, *rest):
    refs, outs = rest[: len(keys)], rest[len(keys) :]
    for ref, (names, offset, stride) in zip(refs, keys):
        _, times, rows, cols = ref.shape
        for at, (aux_bits, orb_bits) in enumerate(names):
            row = pl.multiple_of((position[1] ^ orb_bits) * stride + offset, rows)
            col = pl.multiple_of((position[0] ^ aux_bits) % span * cols, cols)
            for time in range(times):
                high, low = halves(ref[at, time])
                outs[2 * time][pl.ds(row, rows), pl.ds(col, cols)] = high
                outs[2 * time + 1][pl.ds(row, rows), pl.ds(col, cols)] = low


def place(position, gathers, orbitals, span):
    arrays, keys, offset = [], [], 0
    stride = sum(g.arrays()[0].shape[2] for g in gathers)
    for g in gathers:
        arrays += g.arrays()
        keys += [(names, offset, stride) for names in g.keys()]
        offset += g.arrays()[0].shape[2]
    _, times, _, cols = arrays[0].shape
    shape = jax.ShapeDtypeStruct((orbitals, span * cols), jnp.bfloat16)
    return pl.pallas_call(
        functools.partial(place_kernel, keys, span),
        out_shape=[shape] * (2 * times),
        in_specs=[SMEM] + [VMEM] * len(arrays),
        out_specs=[VMEM] * (2 * times),
        compiler_params=PARAMS,
        cost_estimate=cost(8 * orbitals * orbitals, 12 * orbitals * orbitals),
        name="place",
    )(position, *arrays)


def full_kernel(split, a_high, a_low, received, *rest):
    out, b_high, b_low = rest[-3:]
    units, share, block, _ = received.shape
    for source in range(units):
        rows = slice(source // split * block, (source // split + 1) * block)
        for at in range(share):
            col = (source % split * share + at) * block
            b_high[rows, col : col + block], b_low[rows, col : col + block] = halves(received[source, at])
    orbitals = a_high.shape[0]
    tile = 2 * block
    for start in range(0, orbitals, tile):
        rows = slice(start, start + tile)
        product = three_products(a_high[rows], a_low[rows], b_high[...], b_low[...])
        for at in range(share * split):
            out[0, at, 0, rows] = product[:, at * block : (at + 1) * block]


def full_products(vir, received, time, times, split, earlier):
    high, low = vir
    orbitals = high.shape[0]
    units, share, block, _ = received.shape
    aux_count = share * split
    operands = [high, low, received]
    in_specs = [VMEM] * 3
    aliases = {}
    if earlier is not None:
        aliases = {len(operands): 0}
        operands.append(earlier)
        in_specs.append(pl.BlockSpec(memory_space=pl.ANY))
    return pl.pallas_call(
        functools.partial(full_kernel, split),
        grid=(1,),
        out_shape=jax.ShapeDtypeStruct((times, aux_count, 1, orbitals, block), jnp.float32),
        in_specs=in_specs,
        out_specs=pl.BlockSpec((1, aux_count, 1, orbitals, block), lambda i: (time, 0, 0, 0, 0)),
        scratch_shapes=[pltpu.VMEM((orbitals, aux_count * block), jnp.bfloat16)] * 2,
        input_output_aliases=aliases,
        compiler_params=PARAMS,
        cost_estimate=cost(6 * aux_count * block * orbitals * orbitals, 12 * orbitals * orbitals),
        name="full_products",
    )(*operands)


def local(three_center, tile_lists, occ_density, vir_density):
    integrals = three_center.reshape(three_center.shape[0], *three_center.shape[2:])
    block, orbitals = three_center.shape[2:]
    owners, n_aux = lax.axis_size("orb"), lax.axis_size("aux")
    split = owners // (orbitals // block)
    unit = lax.axis_index("orb")
    position = jnp.stack([lax.axis_index("aux"), unit]).astype(jnp.int32)
    times = occ_density.shape[0]
    orb_bits, aux_bits = bits_of(owners), bits_of(n_aux)
    core_bit, far_bits = aux_bits[-1], aux_bits[:-1]

    listed = listed_mask(tile_lists, unit % split, unit // split)
    a_split = split_integrals(listed, integrals)

    half_rows = occ_density.shape[1] // 2

    def begin(value):
        return Gather([(value[None], [(0, 0)])])

    def products(sources, time):
        pair = a_split[2 * time : 2 * time + 2]
        return half_products(position, listed, pair, sources, time, split, block)

    def deliver(made):
        return lax.all_to_all(made, "orb", split_axis=0, concat_axis=0, tiled=True)

    far_orb, middle_orb, near_orb = orb_bits[0], orb_bits[1:-1], orb_bits[-1]

    def step(state, at):
        if at == 0:
            begun = state.step(orb_bits=far_orb)
            return begun.rows(0, half_rows), begun.rows(half_rows, 2 * half_rows)
        one, two = state
        for bit in middle_orb if at == 1 else ():
            one = one.step(orb_bits=bit)
        for bit in far_bits if at == 1 else ():
            two = two.step(aux_bits=bit)
        for bit in middle_orb if at == 2 else ():
            two = two.step(orb_bits=bit)
        if at == 2:
            one = one.step(orb_bits=near_orb)
        for bit in far_bits if at == 3 else ():
            one = one.step(aux_bits=bit, stack=False)
        if at == 3:
            two = two.step(orb_bits=near_orb, stack=False)
        if at == 4:
            one, two = one.step(aux_bits=core_bit, stack=False), two.step(aux_bits=core_bit, stack=False)
        return one, two

    def cross(gathered):
        for bit in far_bits:
            gathered = gathered.step(aux_bits=bit, stack=False)
        return gathered

    states = [begin(occ_density[time]) for time in range(times)]
    received = []
    for turn in range(4 + times):
        for time in range(times):
            if 0 <= turn - time <= 4:
                states[time] = step(states[time], turn - time)
        if turn < 4:
            busy = [time for time in range(times) if turn - time >= 0]
            waited = [g for time in busy for g in states[time]]
            if turn == 0:
                waited += a_split
            if turn == 2:
                waited.append(vir)
            found = together(*waited)
            if turn == 0:
                a_split = found[2:]
                vir = begin(vir_density).after(*found[0].arrays()).step(orb_bits=far_orb)
            if turn == 2:
                vir = found[-1]
                for bit in middle_orb:
                    vir = vir.step(orb_bits=bit)
            for at, time in enumerate(busy):
                states[time] = tuple(found[2 * at : 2 * at + 2])
        time = turn - 4
        if time >= 0:
            one, two = states[time]
            sources = [(one, 0, 2 * half_rows), (two, half_rows, 2 * half_rows)]
            made = products(sources, time)
            if time == 0:
                made, vir, *later = together(made, vir, *[g for state in states[1:] for g in state])
                for at in range(1, times):
                    states[at] = tuple(later[2 * at - 2 : 2 * at])
                over = Gather(vir.step(orb_bits=near_orb, stack=False).parts[1:])
                vir = cross(vir)
            if time == times - 1:
                made, vir, over = together(made, vir, over)
                vir = Gather(vir.parts + cross(over).parts).step(aux_bits=core_bit, stack=False)
            received.append(deliver(made))
    virs = place(position, [vir], orbitals, n_aux)
    coupled = None
    for time in range(times):
        pair = virs[2 * time : 2 * time + 2]
        coupled = full_products(pair, received[time], time, times, split, coupled)
    return coupled


def solution(mesh):
    in_specs = (
        P("aux", "orb", None, None),
        P(None, "aux", None, None),
        P(None, "orb", "aux"),
        P(None, "orb", "aux"),
    )
    out_specs = P(None, "aux", "orb", None, None)
    return jax.shard_map(local, mesh=mesh, in_specs=in_specs, out_specs=out_specs, check_vma=False)
```

```python
import functools

import jax
import jax.numpy as jnp
from jax import lax
from jax.experimental import pallas as pl
from jax.experimental.pallas import tpu as pltpu
from jax.sharding import PartitionSpec as P

VMEM_BYTES = 32 * 1024 * 1024
SMEM = pl.BlockSpec(memory_space=pltpu.SMEM)
VMEM = pl.BlockSpec(memory_space=pltpu.VMEM)
PARAMS = pltpu.CompilerParams(vmem_limit_bytes=VMEM_BYTES)


def cost(flops, moved):
    return pl.CostEstimate(flops=flops, bytes_accessed=moved, transcendentals=0)


def listed_mask(tile_lists, part_index, block_index):
    block_table = lax.dynamic_index_in_dim(tile_lists, part_index, 1, keepdims=False)
    listed_row = lax.dynamic_index_in_dim(block_table, block_index, 1, keepdims=False)
    block_ids = jnp.arange(tile_lists.shape[3], dtype=jnp.int32)
    matches = listed_row[:, :, None] == block_ids[None, None, :]
    return jnp.sum(matches.astype(jnp.float32), axis=1)


def halves(value):
    high = value.astype(jnp.bfloat16)
    return high, (value - high.astype(jnp.float32)).astype(jnp.bfloat16)


def three_products(left_high, left_low, right_high, right_low):
    dot = functools.partial(jnp.dot, preferred_element_type=jnp.float32)
    small = dot(left_low, right_high) + dot(left_high, right_low)
    return dot(left_high, right_high) + small


def after(value, *others):
    return lax.optimization_barrier((value, *others))[0]


def permute(value, target):
    n_aux, n_orb = lax.axis_size("aux"), lax.axis_size("orb")
    pairs = []
    for a in range(n_aux):
        for o in range(n_orb):
            to_aux, to_orb = target(a, o)
            pairs.append((a * n_orb + o, to_aux * n_orb + to_orb))
    return lax.ppermute(value, ("aux", "orb"), pairs)


def swap(value, aux_bits=0, orb_bits=0):
    return permute(value, lambda a, o: (a ^ aux_bits, o ^ orb_bits))


def together(*values):
    parts = [value.arrays() if isinstance(value, Gather) else [value] for value in values]
    arrays = list(lax.optimization_barrier(tuple(array for part in parts for array in part)))
    found = []
    for value in values:
        if isinstance(value, Gather):
            found.append(Gather([(arrays.pop(0), keys) for keys in value.keys()]))
        else:
            found.append(arrays.pop(0))
    return found


def bits_of(size):
    return [1 << at for at in reversed(range(size.bit_length() - 1))]


class Gather:
    def __init__(self, parts):
        self.parts = parts

    def step(self, aux_bits=0, orb_bits=0, stack=True):
        parts = list(self.parts)
        for array, keys in self.parts:
            got = swap(array, aux_bits, orb_bits)
            names = [(a ^ aux_bits, o ^ orb_bits if orb_bits else o) for a, o in keys]
            if stack:
                parts = [(jnp.concatenate([array, got], axis=0), keys + names)]
            else:
                parts.append((got, names))
        return Gather(parts)

    def rows(self, start, stop):
        return Gather([(array[:, start:stop], keys) for array, keys in self.parts])

    def at(self, time):
        return Gather([(array[:, time], keys) for array, keys in self.parts])

    def after(self, *others):
        return Gather([(after(array, *others), keys) for array, keys in self.parts])

    def arrays(self):
        return [array for array, _ in self.parts]

    def keys(self):
        return [keys for _, keys in self.parts]


def owner_of(my_orb, key):
    return key[0] if isinstance(key, tuple) else my_orb ^ key


def split_integrals_kernel(listed, integrals, *outs):
    aux_count, block, orbitals = integrals.shape
    for n in range(orbitals // block):
        cols = slice(n * block, (n + 1) * block)
        part = integrals[:, :, cols].reshape(aux_count * block, block)
        for time in range(listed.shape[0]):
            outs[2 * time][:, cols], outs[2 * time + 1][:, cols] = halves(part * listed[time, n])


def split_integrals(listed, integrals):
    aux_count, block, orbitals = integrals.shape
    times = listed.shape[0]
    shape = jax.ShapeDtypeStruct((aux_count * block, orbitals), jnp.bfloat16)
    return pl.pallas_call(
        split_integrals_kernel,
        out_shape=[shape] * (2 * times),
        in_specs=[SMEM, VMEM],
        out_specs=[VMEM] * (2 * times),
        compiler_params=PARAMS,
        cost_estimate=cost(8 * aux_count * block * orbitals, 12 * aux_count * block * orbitals),
        name="split_integrals",
    )(listed, integrals)


def half_kernel(keys, time, split, position, listed, a_high, a_low, *rest):
    refs, (out, b_high, b_low) = rest[: len(keys)], rest[len(keys) :]
    my_aux, my_orb = position[0], position[1]
    _, share, block, _ = out.shape
    for ref, (names, offset, stride) in zip(refs, keys):
        rows, cols = ref.shape[1:]
        for at, (aux_bits, orb_bits) in enumerate(names):
            row = pl.multiple_of(owner_of(my_orb, orb_bits) * stride + offset, rows)
            col = pl.multiple_of((my_aux ^ aux_bits) * cols, cols)
            high, low = halves(ref[at])
            b_high[pl.ds(row, rows), pl.ds(col, cols)] = high
            b_low[pl.ds(row, rows), pl.ds(col, cols)] = low
    width = 2 * block
    for pair in range(b_high.shape[1] // width):
        cols = slice(pair * width, (pair + 1) * width)
        product = three_products(a_high[...], a_low[...], b_high[:, cols], b_low[:, cols])
        for side in range(2):
            column = pair * 2 + side
            part = product[:, side * block : (side + 1) * block] * listed[time, column]
            part = part.reshape(split, share, block, block)
            for h in range(split):
                out[column * split + h] = part[h]


def half_products(position, listed, a_split, sources, time, split, block):
    a_high, a_low = a_split
    rows, orbitals = a_high.shape
    aux_count = rows // block
    shape = (orbitals // block * split, aux_count // split, block, block)
    arrays, keys = [], []
    for gathered, offset, stride in sources:
        for array, names in gathered.parts:
            arrays.append(array)
            keys.append((names, offset, stride))
    return pl.pallas_call(
        functools.partial(half_kernel, keys, time, split),
        out_shape=jax.ShapeDtypeStruct(shape, jnp.float32),
        in_specs=[SMEM, SMEM, VMEM, VMEM] + [VMEM] * len(arrays),
        out_specs=VMEM,
        scratch_shapes=[pltpu.VMEM((orbitals, orbitals), jnp.bfloat16)] * 2,
        compiler_params=PARAMS,
        cost_estimate=cost(6 * aux_count * block * orbitals * orbitals, 10 * orbitals * orbitals),
        name="half_products",
    )(position, listed, a_high, a_low, *arrays)


def place_kernel(keys, span, position, *rest):
    refs, outs = rest[: len(keys)], rest[len(keys) :]
    for ref, (names, offset, stride) in zip(refs, keys):
        _, times, rows, cols = ref.shape
        for at, (aux_bits, orb_bits) in enumerate(names):
            row = pl.multiple_of((position[1] ^ orb_bits) * stride + offset, rows)
            col = pl.multiple_of((position[0] ^ aux_bits) % span * cols, cols)
            for time in range(times):
                high, low = halves(ref[at, time])
                outs[2 * time][pl.ds(row, rows), pl.ds(col, cols)] = high
                outs[2 * time + 1][pl.ds(row, rows), pl.ds(col, cols)] = low


def place(position, gathers, orbitals, span):
    arrays, keys, offset = [], [], 0
    stride = sum(g.arrays()[0].shape[2] for g in gathers)
    for g in gathers:
        arrays += g.arrays()
        keys += [(names, offset, stride) for names in g.keys()]
        offset += g.arrays()[0].shape[2]
    _, times, _, cols = arrays[0].shape
    shape = jax.ShapeDtypeStruct((orbitals, span * cols), jnp.bfloat16)
    return pl.pallas_call(
        functools.partial(place_kernel, keys, span),
        out_shape=[shape] * (2 * times),
        in_specs=[SMEM] + [VMEM] * len(arrays),
        out_specs=[VMEM] * (2 * times),
        compiler_params=PARAMS,
        cost_estimate=cost(8 * orbitals * orbitals, 12 * orbitals * orbitals),
        name="place",
    )(position, *arrays)


def full_kernel(split, a_high, a_low, received, *rest):
    out, b_high, b_low = rest[-3:]
    units, share, block, _ = received.shape
    for source in range(units):
        rows = slice(source // split * block, (source // split + 1) * block)
        for at in range(share):
            col = (source % split * share + at) * block
            b_high[rows, col : col + block], b_low[rows, col : col + block] = halves(received[source, at])
    orbitals = a_high.shape[0]
    tile = 2 * block
    for start in range(0, orbitals, tile):
        rows = slice(start, start + tile)
        product = three_products(a_high[rows], a_low[rows], b_high[...], b_low[...])
        for at in range(share * split):
            out[0, at, 0, rows] = product[:, at * block : (at + 1) * block]


def full_products(vir, received, time, times, split, earlier):
    high, low = vir
    orbitals = high.shape[0]
    units, share, block, _ = received.shape
    aux_count = share * split
    operands = [high, low, received]
    in_specs = [VMEM] * 3
    aliases = {}
    if earlier is not None:
        aliases = {len(operands): 0}
        operands.append(earlier)
        in_specs.append(pl.BlockSpec(memory_space=pl.ANY))
    return pl.pallas_call(
        functools.partial(full_kernel, split),
        grid=(1,),
        out_shape=jax.ShapeDtypeStruct((times, aux_count, 1, orbitals, block), jnp.float32),
        in_specs=in_specs,
        out_specs=pl.BlockSpec((1, aux_count, 1, orbitals, block), lambda i: (time, 0, 0, 0, 0)),
        scratch_shapes=[pltpu.VMEM((orbitals, aux_count * block), jnp.bfloat16)] * 2,
        input_output_aliases=aliases,
        compiler_params=PARAMS,
        cost_estimate=cost(6 * aux_count * block * orbitals * orbitals, 12 * orbitals * orbitals),
        name="full_products",
    )(*operands)


def local(three_center, tile_lists, occ_density, vir_density):
    integrals = three_center.reshape(three_center.shape[0], *three_center.shape[2:])
    block, orbitals = three_center.shape[2:]
    owners, n_aux = lax.axis_size("orb"), lax.axis_size("aux")
    split = owners // (orbitals // block)
    unit = lax.axis_index("orb")
    position = jnp.stack([lax.axis_index("aux"), unit]).astype(jnp.int32)
    times = occ_density.shape[0]
    orb_bits, aux_bits = bits_of(owners), bits_of(n_aux)
    core_bit, far_bits = aux_bits[-1], aux_bits[:-1]

    listed = listed_mask(tile_lists, unit % split, unit // split)
    a_split = split_integrals(listed, integrals)

    half_rows = occ_density.shape[1] // 2

    def begin(value):
        return Gather([(value[None], [(0, 0)])])

    def products(sources, time):
        pair = a_split[2 * time : 2 * time + 2]
        return half_products(position, listed, pair, sources, time, split, block)

    def deliver(made):
        return lax.all_to_all(made, "orb", split_axis=0, concat_axis=0, tiled=True)

    far_orb, middle_orb, near_orb = orb_bits[0], orb_bits[1:-1], orb_bits[-1]

    def step(state, at):
        if at == 0:
            begun = state.step(orb_bits=far_orb)
            return begun.rows(0, half_rows), begun.rows(half_rows, 2 * half_rows)
        one, two = state
        for bit in middle_orb if at == 1 else ():
            one = one.step(orb_bits=bit)
        for bit in far_bits if at == 1 else ():
            two = two.step(aux_bits=bit)
        for bit in middle_orb if at == 2 else ():
            two = two.step(orb_bits=bit)
        if at == 2:
            one = one.step(orb_bits=near_orb)
        for bit in far_bits if at == 3 else ():
            one = one.step(aux_bits=bit, stack=False)
        if at == 3:
            two = two.step(orb_bits=near_orb, stack=False)
        if at == 4:
            one, two = one.step(aux_bits=core_bit, stack=False), two.step(aux_bits=core_bit, stack=False)
        return one, two

    def cross(gathered):
        for bit in far_bits:
            gathered = gathered.step(aux_bits=bit, stack=False)
        return gathered

    states = [begin(occ_density[time]) for time in range(times)]
    received = []
    for turn in range(4 + times):
        for time in range(times):
            if 0 <= turn - time <= 4:
                states[time] = step(states[time], turn - time)
        if turn < 4:
            busy = [time for time in range(times) if turn - time >= 0]
            waited = [g for time in busy for g in states[time]]
            if turn == 0:
                waited += a_split
            if turn == 2:
                waited.append(vir)
            found = together(*waited)
            if turn == 0:
                a_split = found[2:]
                states[1:] = [state.after(*found[0].arrays()) for state in states[1:]]
                vir = begin(vir_density).after(*found[0].arrays()).step(orb_bits=far_orb)
            if turn == 2:
                vir = found[-1]
                for bit in middle_orb:
                    vir = vir.step(orb_bits=bit)
            for at, time in enumerate(busy):
                states[time] = tuple(found[2 * at : 2 * at + 2])
        time = turn - 4
        if time >= 0:
            one, two = states[time]
            sources = [(one, 0, 2 * half_rows), (two, half_rows, 2 * half_rows)]
            made = products(sources, time)
            if time == 0:
                made, vir, *later = together(made, vir, *[g for state in states[1:] for g in state])
                for at in range(1, times):
                    states[at] = tuple(later[2 * at - 2 : 2 * at])
                over = Gather(vir.step(orb_bits=near_orb, stack=False).parts[1:])
                vir = cross(vir)
            if time == times - 1:
                made, vir, over = together(made, vir, over)
                vir = Gather(vir.parts + cross(over).parts).step(aux_bits=core_bit, stack=False)
            received.append(deliver(made))
    virs = place(position, [vir], orbitals, n_aux)
    coupled = None
    for time in range(times):
        pair = virs[2 * time : 2 * time + 2]
        coupled = full_products(pair, received[time], time, times, split, coupled)
    return coupled


def solution(mesh):
    in_specs = (
        P("aux", "orb", None, None),
        P(None, "aux", None, None),
        P(None, "orb", "aux"),
        P(None, "orb", "aux"),
    )
    out_specs = P(None, "aux", "orb", None, None)
    return jax.shard_map(local, mesh=mesh, in_specs=in_specs, out_specs=out_specs, check_vma=False)
```

```python
import functools

import jax
import jax.numpy as jnp
from jax import lax
from jax.experimental import pallas as pl
from jax.experimental.pallas import tpu as pltpu
from jax.sharding import PartitionSpec as P

VMEM_BYTES = 32 * 1024 * 1024
SMEM = pl.BlockSpec(memory_space=pltpu.SMEM)
VMEM = pl.BlockSpec(memory_space=pltpu.VMEM)
PARAMS = pltpu.CompilerParams(vmem_limit_bytes=VMEM_BYTES)


def cost(flops, moved):
    return pl.CostEstimate(flops=flops, bytes_accessed=moved, transcendentals=0)


def listed_mask(tile_lists, part_index, block_index):
    block_table = lax.dynamic_index_in_dim(tile_lists, part_index, 1, keepdims=False)
    listed_row = lax.dynamic_index_in_dim(block_table, block_index, 1, keepdims=False)
    block_ids = jnp.arange(tile_lists.shape[3], dtype=jnp.int32)
    matches = listed_row[:, :, None] == block_ids[None, None, :]
    return jnp.sum(matches.astype(jnp.float32), axis=1)


def halves(value):
    high = value.astype(jnp.bfloat16)
    return high, (value - high.astype(jnp.float32)).astype(jnp.bfloat16)


def three_products(left_high, left_low, right_high, right_low):
    dot = functools.partial(jnp.dot, preferred_element_type=jnp.float32)
    small = dot(left_low, right_high) + dot(left_high, right_low)
    return dot(left_high, right_high) + small


def after(value, *others):
    return lax.optimization_barrier((value, *others))[0]


def permute(value, target):
    n_aux, n_orb = lax.axis_size("aux"), lax.axis_size("orb")
    pairs = []
    for a in range(n_aux):
        for o in range(n_orb):
            to_aux, to_orb = target(a, o)
            pairs.append((a * n_orb + o, to_aux * n_orb + to_orb))
    return lax.ppermute(value, ("aux", "orb"), pairs)


def swap(value, aux_bits=0, orb_bits=0):
    return permute(value, lambda a, o: (a ^ aux_bits, o ^ orb_bits))


def together(*values):
    parts = [value.arrays() if isinstance(value, Gather) else [value] for value in values]
    arrays = list(lax.optimization_barrier(tuple(array for part in parts for array in part)))
    found = []
    for value in values:
        if isinstance(value, Gather):
            found.append(Gather([(arrays.pop(0), keys) for keys in value.keys()]))
        else:
            found.append(arrays.pop(0))
    return found


def bits_of(size):
    return [1 << at for at in reversed(range(size.bit_length() - 1))]


class Gather:
    def __init__(self, parts):
        self.parts = parts

    def step(self, aux_bits=0, orb_bits=0, stack=True):
        parts = list(self.parts)
        for array, keys in self.parts:
            got = swap(array, aux_bits, orb_bits)
            names = [(a ^ aux_bits, o ^ orb_bits if orb_bits else o) for a, o in keys]
            if stack:
                parts = [(jnp.concatenate([array, got], axis=0), keys + names)]
            else:
                parts.append((got, names))
        return Gather(parts)

    def rows(self, start, stop):
        return Gather([(array[:, start:stop], keys) for array, keys in self.parts])

    def at(self, time):
        return Gather([(array[:, time], keys) for array, keys in self.parts])

    def after(self, *others):
        return Gather([(after(array, *others), keys) for array, keys in self.parts])

    def arrays(self):
        return [array for array, _ in self.parts]

    def keys(self):
        return [keys for _, keys in self.parts]


def owner_of(my_orb, key):
    return key[0] if isinstance(key, tuple) else my_orb ^ key


def split_integrals_kernel(listed, integrals, *outs):
    aux_count, block, orbitals = integrals.shape
    for n in range(orbitals // block):
        cols = slice(n * block, (n + 1) * block)
        part = integrals[:, :, cols].reshape(aux_count * block, block)
        for time in range(listed.shape[0]):
            outs[2 * time][:, cols], outs[2 * time + 1][:, cols] = halves(part * listed[time, n])


def split_integrals(listed, integrals):
    aux_count, block, orbitals = integrals.shape
    times = listed.shape[0]
    shape = jax.ShapeDtypeStruct((aux_count * block, orbitals), jnp.bfloat16)
    return pl.pallas_call(
        split_integrals_kernel,
        out_shape=[shape] * (2 * times),
        in_specs=[SMEM, VMEM],
        out_specs=[VMEM] * (2 * times),
        compiler_params=PARAMS,
        cost_estimate=cost(8 * aux_count * block * orbitals, 12 * aux_count * block * orbitals),
        name="split_integrals",
    )(listed, integrals)


def half_kernel(keys, time, split, position, listed, a_high, a_low, *rest):
    refs, (out, b_high, b_low) = rest[: len(keys)], rest[len(keys) :]
    my_aux, my_orb = position[0], position[1]
    _, share, block, _ = out.shape
    for ref, (names, offset, stride) in zip(refs, keys):
        rows, cols = ref.shape[1:]
        for at, (aux_bits, orb_bits) in enumerate(names):
            row = pl.multiple_of(owner_of(my_orb, orb_bits) * stride + offset, rows)
            col = pl.multiple_of((my_aux ^ aux_bits) * cols, cols)
            high, low = halves(ref[at])
            b_high[pl.ds(row, rows), pl.ds(col, cols)] = high
            b_low[pl.ds(row, rows), pl.ds(col, cols)] = low
    width = 2 * block
    for pair in range(b_high.shape[1] // width):
        cols = slice(pair * width, (pair + 1) * width)
        product = three_products(a_high[...], a_low[...], b_high[:, cols], b_low[:, cols])
        for side in range(2):
            column = pair * 2 + side
            part = product[:, side * block : (side + 1) * block] * listed[time, column]
            part = part.reshape(split, share, block, block)
            for h in range(split):
                out[column * split + h] = part[h]


def half_products(position, listed, a_split, sources, time, split, block):
    a_high, a_low = a_split
    rows, orbitals = a_high.shape
    aux_count = rows // block
    shape = (orbitals // block * split, aux_count // split, block, block)
    arrays, keys = [], []
    for gathered, offset, stride in sources:
        for array, names in gathered.parts:
            arrays.append(array)
            keys.append((names, offset, stride))
    return pl.pallas_call(
        functools.partial(half_kernel, keys, time, split),
        out_shape=jax.ShapeDtypeStruct(shape, jnp.float32),
        in_specs=[SMEM, SMEM, VMEM, VMEM] + [VMEM] * len(arrays),
        out_specs=VMEM,
        scratch_shapes=[pltpu.VMEM((orbitals, orbitals), jnp.bfloat16)] * 2,
        compiler_params=PARAMS,
        cost_estimate=cost(6 * aux_count * block * orbitals * orbitals, 10 * orbitals * orbitals),
        name="half_products",
    )(position, listed, a_high, a_low, *arrays)


def place_kernel(keys, span, position, *rest):
    refs, outs = rest[: len(keys)], rest[len(keys) :]
    for ref, (names, offset, stride) in zip(refs, keys):
        _, times, rows, cols = ref.shape
        for at, (aux_bits, orb_bits) in enumerate(names):
            row = pl.multiple_of((position[1] ^ orb_bits) * stride + offset, rows)
            col = pl.multiple_of((position[0] ^ aux_bits) % span * cols, cols)
            for time in range(times):
                high, low = halves(ref[at, time])
                outs[2 * time][pl.ds(row, rows), pl.ds(col, cols)] = high
                outs[2 * time + 1][pl.ds(row, rows), pl.ds(col, cols)] = low


def place(position, gathers, orbitals, span):
    arrays, keys, offset = [], [], 0
    stride = sum(g.arrays()[0].shape[2] for g in gathers)
    for g in gathers:
        arrays += g.arrays()
        keys += [(names, offset, stride) for names in g.keys()]
        offset += g.arrays()[0].shape[2]
    _, times, _, cols = arrays[0].shape
    shape = jax.ShapeDtypeStruct((orbitals, span * cols), jnp.bfloat16)
    return pl.pallas_call(
        functools.partial(place_kernel, keys, span),
        out_shape=[shape] * (2 * times),
        in_specs=[SMEM] + [VMEM] * len(arrays),
        out_specs=[VMEM] * (2 * times),
        compiler_params=PARAMS,
        cost_estimate=cost(8 * orbitals * orbitals, 12 * orbitals * orbitals),
        name="place",
    )(position, *arrays)


def full_kernel(split, a_high, a_low, received, *rest):
    out, b_high, b_low = rest[-3:]
    units, share, block, _ = received.shape

    @pl.when(pl.program_id(0) == 0)
    def _():
        for source in range(units):
            rows = slice(source // split * block, (source // split + 1) * block)
            for at in range(share):
                col = (source % split * share + at) * block
                high, low = halves(received[source, at])
                b_high[rows, col : col + block], b_low[rows, col : col + block] = high, low

    product = three_products(a_high[...], a_low[...], b_high[...], b_low[...])
    for at in range(share * split):
        out[0, at, 0] = product[:, at * block : (at + 1) * block]


def full_products(vir, received, time, times, split, earlier):
    high, low = vir
    orbitals = high.shape[0]
    units, share, block, _ = received.shape
    aux_count = share * split
    tile = 2 * block
    operands = [high, low, received]
    some_rows = pl.BlockSpec((tile, orbitals), lambda i: (i, 0))
    in_specs = [some_rows, some_rows, VMEM]
    aliases = {}
    if earlier is not None:
        aliases = {len(operands): 0}
        operands.append(earlier)
        in_specs.append(pl.BlockSpec(memory_space=pl.ANY))
    return pl.pallas_call(
        functools.partial(full_kernel, split),
        grid=(orbitals // tile,),
        out_shape=jax.ShapeDtypeStruct((times, aux_count, 1, orbitals, block), jnp.float32),
        in_specs=in_specs,
        out_specs=pl.BlockSpec((1, aux_count, 1, tile, block), lambda i: (time, 0, 0, i, 0)),
        scratch_shapes=[pltpu.VMEM((orbitals, aux_count * block), jnp.bfloat16)] * 2,
        input_output_aliases=aliases,
        compiler_params=pltpu.CompilerParams(vmem_limit_bytes=52 * 1024 * 1024),
        cost_estimate=cost(6 * aux_count * block * orbitals * orbitals, 12 * orbitals * orbitals),
        name="full_products",
    )(*operands)


def local(three_center, tile_lists, occ_density, vir_density):
    integrals = three_center.reshape(three_center.shape[0], *three_center.shape[2:])
    block, orbitals = three_center.shape[2:]
    owners, n_aux = lax.axis_size("orb"), lax.axis_size("aux")
    split = owners // (orbitals // block)
    unit = lax.axis_index("orb")
    position = jnp.stack([lax.axis_index("aux"), unit]).astype(jnp.int32)
    times = occ_density.shape[0]
    orb_bits, aux_bits = bits_of(owners), bits_of(n_aux)
    core_bit, far_bits = aux_bits[-1], aux_bits[:-1]

    listed = listed_mask(tile_lists, unit % split, unit // split)
    a_split = split_integrals(listed, integrals)

    half_rows = occ_density.shape[1] // 2

    def begin(value):
        return Gather([(value[None], [(0, 0)])])

    def products(sources, time):
        pair = a_split[2 * time : 2 * time + 2]
        return half_products(position, listed, pair, sources, time, split, block)

    def deliver(made):
        return lax.all_to_all(made, "orb", split_axis=0, concat_axis=0, tiled=True)

    far_orb, middle_orb, near_orb = orb_bits[0], orb_bits[1:-1], orb_bits[-1]

    def step(state, at):
        if at == 0:
            begun = state.step(orb_bits=far_orb)
            return begun.rows(0, half_rows), begun.rows(half_rows, 2 * half_rows)
        one, two = state
        for bit in middle_orb if at == 1 else ():
            one = one.step(orb_bits=bit)
        for bit in far_bits if at == 1 else ():
            two = two.step(aux_bits=bit)
        for bit in middle_orb if at == 2 else ():
            two = two.step(orb_bits=bit)
        if at == 2:
            one = one.step(orb_bits=near_orb)
        for bit in far_bits if at == 3 else ():
            one = one.step(aux_bits=bit, stack=False)
        if at == 3:
            two = two.step(orb_bits=near_orb, stack=False)
        if at == 4:
            one, two = one.step(aux_bits=core_bit, stack=False), two.step(aux_bits=core_bit, stack=False)
        return one, two

    def cross(gathered):
        for bit in far_bits:
            gathered = gathered.step(aux_bits=bit, stack=False)
        return gathered

    states = [begin(occ_density[time]) for time in range(times)]
    received = []
    for turn in range(4 + times):
        for time in range(times):
            if 0 <= turn - time <= 4:
                states[time] = step(states[time], turn - time)
        if turn < 4:
            busy = [time for time in range(times) if turn - time >= 0]
            waited = [g for time in busy for g in states[time]]
            if turn == 0:
                waited += a_split
            if turn == 2:
                waited.append(vir)
            found = together(*waited)
            if turn == 0:
                a_split = found[2:]
                states[1:] = [state.after(*found[0].arrays()) for state in states[1:]]
                vir = begin(vir_density).after(*found[0].arrays()).step(orb_bits=far_orb)
            if turn == 2:
                vir = found[-1]
                for bit in middle_orb:
                    vir = vir.step(orb_bits=bit)
            for at, time in enumerate(busy):
                states[time] = tuple(found[2 * at : 2 * at + 2])
        time = turn - 4
        if time >= 0:
            one, two = states[time]
            sources = [(one, 0, 2 * half_rows), (two, half_rows, 2 * half_rows)]
            made = products(sources, time)
            if time == 0:
                made, vir, *later = together(made, vir, *[g for state in states[1:] for g in state])
                for at in range(1, times):
                    states[at] = tuple(later[2 * at - 2 : 2 * at])
                over = Gather(vir.step(orb_bits=near_orb, stack=False).parts[1:])
                vir = cross(vir)
            if time == times - 1:
                made, vir, over = together(made, vir, over)
                vir = Gather(vir.parts + cross(over).parts).step(aux_bits=core_bit, stack=False)
            received.append(deliver(made))
    virs = place(position, [vir], orbitals, n_aux)
    coupled = None
    for time in range(times):
        pair = virs[2 * time : 2 * time + 2]
        coupled = full_products(pair, received[time], time, times, split, coupled)
    return coupled


def solution(mesh):
    in_specs = (
        P("aux", "orb", None, None),
        P(None, "aux", None, None),
        P(None, "orb", "aux"),
        P(None, "orb", "aux"),
    )
    out_specs = P(None, "aux", "orb", None, None)
    return jax.shard_map(local, mesh=mesh, in_specs=in_specs, out_specs=out_specs, check_vma=False)
```

```python
import functools

import jax
import jax.numpy as jnp
from jax import lax
from jax.experimental import pallas as pl
from jax.experimental.pallas import tpu as pltpu
from jax.sharding import PartitionSpec as P

VMEM_BYTES = 32 * 1024 * 1024
SMEM = pl.BlockSpec(memory_space=pltpu.SMEM)
VMEM = pl.BlockSpec(memory_space=pltpu.VMEM)
PARAMS = pltpu.CompilerParams(vmem_limit_bytes=VMEM_BYTES)


def cost(flops, moved):
    return pl.CostEstimate(flops=flops, bytes_accessed=moved, transcendentals=0)


def listed_mask(tile_lists, part_index, block_index):
    block_table = lax.dynamic_index_in_dim(tile_lists, part_index, 1, keepdims=False)
    listed_row = lax.dynamic_index_in_dim(block_table, block_index, 1, keepdims=False)
    block_ids = jnp.arange(tile_lists.shape[3], dtype=jnp.int32)
    matches = listed_row[:, :, None] == block_ids[None, None, :]
    return jnp.sum(matches.astype(jnp.float32), axis=1)


def halves(value):
    high = value.astype(jnp.bfloat16)
    return high, (value - high.astype(jnp.float32)).astype(jnp.bfloat16)


def three_products(left_high, left_low, right_high, right_low):
    dot = functools.partial(jnp.dot, preferred_element_type=jnp.float32)
    small = dot(left_low, right_high) + dot(left_high, right_low)
    return dot(left_high, right_high) + small


def after(value, *others):
    return lax.optimization_barrier((value, *others))[0]


def permute(value, target):
    n_aux, n_orb = lax.axis_size("aux"), lax.axis_size("orb")
    pairs = []
    for a in range(n_aux):
        for o in range(n_orb):
            to_aux, to_orb = target(a, o)
            pairs.append((a * n_orb + o, to_aux * n_orb + to_orb))
    return lax.ppermute(value, ("aux", "orb"), pairs)


def swap(value, aux_bits=0, orb_bits=0):
    return permute(value, lambda a, o: (a ^ aux_bits, o ^ orb_bits))


def together(*values):
    parts = [value.arrays() if isinstance(value, Gather) else [value] for value in values]
    arrays = list(lax.optimization_barrier(tuple(array for part in parts for array in part)))
    found = []
    for value in values:
        if isinstance(value, Gather):
            found.append(Gather([(arrays.pop(0), keys) for keys in value.keys()]))
        else:
            found.append(arrays.pop(0))
    return found


def bits_of(size):
    return [1 << at for at in reversed(range(size.bit_length() - 1))]


class Gather:
    def __init__(self, parts):
        self.parts = parts

    def step(self, aux_bits=0, orb_bits=0, stack=True):
        parts = list(self.parts)
        for array, keys in self.parts:
            got = swap(array, aux_bits, orb_bits)
            names = [(a ^ aux_bits, o ^ orb_bits if orb_bits else o) for a, o in keys]
            if stack:
                parts = [(jnp.concatenate([array, got], axis=0), keys + names)]
            else:
                parts.append((got, names))
        return Gather(parts)

    def rows(self, start, stop):
        return Gather([(array[:, start:stop], keys) for array, keys in self.parts])

    def at(self, time):
        return Gather([(array[:, time], keys) for array, keys in self.parts])

    def after(self, *others):
        return Gather([(after(array, *others), keys) for array, keys in self.parts])

    def arrays(self):
        return [array for array, _ in self.parts]

    def keys(self):
        return [keys for _, keys in self.parts]


def owner_of(my_orb, key):
    return key[0] if isinstance(key, tuple) else my_orb ^ key


def split_integrals_kernel(listed, integrals, *outs):
    aux_count, block, orbitals = integrals.shape
    for n in range(orbitals // block):
        cols = slice(n * block, (n + 1) * block)
        part = integrals[:, :, cols].reshape(aux_count * block, block)
        for time in range(listed.shape[0]):
            outs[2 * time][:, cols], outs[2 * time + 1][:, cols] = halves(part * listed[time, n])


def split_integrals(listed, integrals):
    aux_count, block, orbitals = integrals.shape
    times = listed.shape[0]
    shape = jax.ShapeDtypeStruct((aux_count * block, orbitals), jnp.bfloat16)
    return pl.pallas_call(
        split_integrals_kernel,
        out_shape=[shape] * (2 * times),
        in_specs=[SMEM, VMEM],
        out_specs=[VMEM] * (2 * times),
        compiler_params=PARAMS,
        cost_estimate=cost(8 * aux_count * block * orbitals, 12 * aux_count * block * orbitals),
        name="split_integrals",
    )(listed, integrals)


def half_kernel(keys, time, split, position, listed, a_high, a_low, *rest):
    refs, (out, b_high, b_low) = rest[: len(keys)], rest[len(keys) :]
    my_aux, my_orb = position[0], position[1]
    _, share, block, _ = out.shape
    for ref, (names, offset, stride) in zip(refs, keys):
        rows, cols = ref.shape[1:]
        for at, (aux_bits, orb_bits) in enumerate(names):
            row = pl.multiple_of(owner_of(my_orb, orb_bits) * stride + offset, rows)
            col = pl.multiple_of((my_aux ^ aux_bits) * cols, cols)
            high, low = halves(ref[at])
            b_high[pl.ds(row, rows), pl.ds(col, cols)] = high
            b_low[pl.ds(row, rows), pl.ds(col, cols)] = low
    width = 2 * block
    for pair in range(b_high.shape[1] // width):
        cols = slice(pair * width, (pair + 1) * width)
        product = three_products(a_high[...], a_low[...], b_high[:, cols], b_low[:, cols])
        for side in range(2):
            column = pair * 2 + side
            part = product[:, side * block : (side + 1) * block] * listed[time, column]
            part = part.reshape(split, share, block, block)
            for h in range(split):
                out[column * split + h] = part[h]


def half_products(position, listed, a_split, sources, time, split, block):
    a_high, a_low = a_split
    rows, orbitals = a_high.shape
    aux_count = rows // block
    shape = (orbitals // block * split, aux_count // split, block, block)
    arrays, keys = [], []
    for gathered, offset, stride in sources:
        for array, names in gathered.parts:
            arrays.append(array)
            keys.append((names, offset, stride))
    return pl.pallas_call(
        functools.partial(half_kernel, keys, time, split),
        out_shape=jax.ShapeDtypeStruct(shape, jnp.float32),
        in_specs=[SMEM, SMEM, VMEM, VMEM] + [VMEM] * len(arrays),
        out_specs=VMEM,
        scratch_shapes=[pltpu.VMEM((orbitals, orbitals), jnp.bfloat16)] * 2,
        compiler_params=pltpu.CompilerParams(vmem_limit_bytes=56 * 1024 * 1024),
        cost_estimate=cost(6 * aux_count * block * orbitals * orbitals, 10 * orbitals * orbitals),
        name="half_products",
    )(position, listed, a_high, a_low, *arrays)


def place_kernel(keys, span, position, *rest):
    refs, outs = rest[: len(keys)], rest[len(keys) :]
    for ref, (names, offset, stride) in zip(refs, keys):
        _, times, rows, cols = ref.shape
        for at, (aux_bits, orb_bits) in enumerate(names):
            row = pl.multiple_of((position[1] ^ orb_bits) * stride + offset, rows)
            col = pl.multiple_of((position[0] ^ aux_bits) % span * cols, cols)
            for time in range(times):
                high, low = halves(ref[at, time])
                outs[2 * time][pl.ds(row, rows), pl.ds(col, cols)] = high
                outs[2 * time + 1][pl.ds(row, rows), pl.ds(col, cols)] = low


def place(position, gathers, orbitals, span):
    arrays, keys, offset = [], [], 0
    stride = sum(g.arrays()[0].shape[2] for g in gathers)
    for g in gathers:
        arrays += g.arrays()
        keys += [(names, offset, stride) for names in g.keys()]
        offset += g.arrays()[0].shape[2]
    _, times, _, cols = arrays[0].shape
    shape = jax.ShapeDtypeStruct((orbitals, span * cols), jnp.bfloat16)
    return pl.pallas_call(
        functools.partial(place_kernel, keys, span),
        out_shape=[shape] * (2 * times),
        in_specs=[SMEM] + [VMEM] * len(arrays),
        out_specs=[VMEM] * (2 * times),
        compiler_params=PARAMS,
        cost_estimate=cost(8 * orbitals * orbitals, 12 * orbitals * orbitals),
        name="place",
    )(position, *arrays)


def full_kernel(split, a_high, a_low, received, *rest):
    out, b_high, b_low = rest[-3:]
    units, share, block, _ = received.shape

    @pl.when(pl.program_id(0) == 0)
    def _():
        for source in range(units):
            rows = slice(source // split * block, (source // split + 1) * block)
            for at in range(share):
                col = (source % split * share + at) * block
                high, low = halves(received[source, at])
                b_high[rows, col : col + block], b_low[rows, col : col + block] = high, low

    product = three_products(a_high[...], a_low[...], b_high[...], b_low[...])
    for at in range(share * split):
        out[0, at, 0] = product[:, at * block : (at + 1) * block]


def full_products(vir, received, time, times, split, earlier):
    high, low = vir
    orbitals = high.shape[0]
    units, share, block, _ = received.shape
    aux_count = share * split
    tile = 2 * block
    operands = [high, low, received]
    some_rows = pl.BlockSpec((tile, orbitals), lambda i: (i, 0))
    in_specs = [some_rows, some_rows, VMEM]
    aliases = {}
    if earlier is not None:
        aliases = {len(operands): 0}
        operands.append(earlier)
        in_specs.append(pl.BlockSpec(memory_space=pl.ANY))
    return pl.pallas_call(
        functools.partial(full_kernel, split),
        grid=(orbitals // tile,),
        out_shape=jax.ShapeDtypeStruct((times, aux_count, 1, orbitals, block), jnp.float32),
        in_specs=in_specs,
        out_specs=pl.BlockSpec((1, aux_count, 1, tile, block), lambda i: (time, 0, 0, i, 0)),
        scratch_shapes=[pltpu.VMEM((orbitals, aux_count * block), jnp.bfloat16)] * 2,
        input_output_aliases=aliases,
        compiler_params=pltpu.CompilerParams(vmem_limit_bytes=52 * 1024 * 1024),
        cost_estimate=cost(6 * aux_count * block * orbitals * orbitals, 12 * orbitals * orbitals),
        name="full_products",
    )(*operands)


def local(three_center, tile_lists, occ_density, vir_density):
    integrals = three_center.reshape(three_center.shape[0], *three_center.shape[2:])
    block, orbitals = three_center.shape[2:]
    owners, n_aux = lax.axis_size("orb"), lax.axis_size("aux")
    split = owners // (orbitals // block)
    unit = lax.axis_index("orb")
    position = jnp.stack([lax.axis_index("aux"), unit]).astype(jnp.int32)
    times = occ_density.shape[0]
    orb_bits, aux_bits = bits_of(owners), bits_of(n_aux)
    core_bit, far_bits = aux_bits[-1], aux_bits[:-1]

    listed = listed_mask(tile_lists, unit % split, unit // split)
    a_split = split_integrals(listed, integrals)

    half_rows = occ_density.shape[1] // 2

    def begin(value):
        return Gather([(value[None], [(0, 0)])])

    def products(sources, time):
        pair = a_split[2 * time : 2 * time + 2]
        return half_products(position, listed, pair, sources, time, split, block)

    def deliver(made):
        return lax.all_to_all(made, "orb", split_axis=0, concat_axis=0, tiled=True)

    far_orb, middle_orb, near_orb = orb_bits[0], orb_bits[1:-1], orb_bits[-1]

    def step(state, at):
        if at == 0:
            begun = state.step(orb_bits=far_orb)
            return begun.rows(0, half_rows), begun.rows(half_rows, 2 * half_rows)
        one, two = state
        for bit in middle_orb if at == 1 else ():
            one = one.step(orb_bits=bit)
        for bit in far_bits if at == 1 else ():
            two = two.step(aux_bits=bit)
        for bit in middle_orb if at == 2 else ():
            two = two.step(orb_bits=bit)
        if at == 2:
            one = one.step(orb_bits=near_orb)
        for bit in far_bits if at == 3 else ():
            one = one.step(aux_bits=bit, stack=False)
        if at == 3:
            two = two.step(orb_bits=near_orb, stack=False)
        if at == 4:
            one, two = one.step(aux_bits=core_bit, stack=False), two.step(aux_bits=core_bit, stack=False)
        return one, two

    def cross(gathered):
        for bit in far_bits:
            gathered = gathered.step(aux_bits=bit, stack=False)
        return gathered

    states = [begin(occ_density[time]) for time in range(times)]
    received = []
    for turn in range(4 + times):
        for time in range(times):
            if 0 <= turn - time <= 4:
                states[time] = step(states[time], turn - time)
        if turn < 4:
            busy = [time for time in range(times) if turn - time >= 0]
            waited = [g for time in busy for g in states[time]]
            if turn == 0:
                waited += a_split
            if turn == 2:
                waited.append(vir)
            found = together(*waited)
            if turn == 0:
                a_split = found[2:]
                states[1:] = [state.after(*found[0].arrays()) for state in states[1:]]
                vir = begin(vir_density).after(*found[0].arrays()).step(orb_bits=far_orb)
            if turn == 2:
                vir = found[-1]
                for bit in middle_orb:
                    vir = vir.step(orb_bits=bit)
            for at, time in enumerate(busy):
                states[time] = tuple(found[2 * at : 2 * at + 2])
        time = turn - 4
        if time >= 0:
            one, two = states[time]
            sources = [(one, 0, 2 * half_rows), (two, half_rows, 2 * half_rows)]
            made = products(sources, time)
            if time == 0:
                made, vir, *later = together(made, vir, *[g for state in states[1:] for g in state])
                for at in range(1, times):
                    states[at] = tuple(later[2 * at - 2 : 2 * at])
                over = Gather(vir.step(orb_bits=near_orb, stack=False).parts[1:])
                vir = cross(vir)
            if time == times - 1:
                made, vir, over = together(made, vir, over)
                vir = Gather(vir.parts + cross(over).parts).step(aux_bits=core_bit, stack=False)
            received.append(deliver(made))
    virs = place(position, [vir], orbitals, n_aux)
    coupled = None
    for time in range(times):
        pair = virs[2 * time : 2 * time + 2]
        coupled = full_products(pair, received[time], time, times, split, coupled)
    return coupled


def solution(mesh):
    in_specs = (
        P("aux", "orb", None, None),
        P(None, "aux", None, None),
        P(None, "orb", "aux"),
        P(None, "orb", "aux"),
    )
    out_specs = P(None, "aux", "orb", None, None)
    return jax.shard_map(local, mesh=mesh, in_specs=in_specs, out_specs=out_specs, check_vma=False)
```
